128 devices in a mesh: row: 8 (over y, z_hi), col: 16 (over z_lo, x, core).
Axes of the slice: x: 4, y: 4, z: 4 (z_hi: 2, z_lo: 2; z = z_hi * 2 + z_lo), core: 2. Of those that a mesh axis runs over, the one named last changes fastest.
Arguments:
- acts: bfloat16 [2048, 12288], P('row', 'col'), may hold values from -6 to 6
- weight: bfloat16 [12288, 24576], P('col', 'row'), may hold values from -0.0546875 to 0.0546875
- cotangent: bfloat16 [2048, 24576], P('col', 'row'), may hold values from -1.1953125 to 1.1953125
Outputs:
- hidden: bfloat16 [2048, 24576], P('col', 'row')
- grad_acts: bfloat16 [2048, 12288], P('row', 'col')
- grad_weight: bfloat16 [12288, 24576], P('col', 'row')
The draws below stay inside these ranges and needn't reach their ends.
All inputs are finite; a program needn't handle non-finite values.
Results may differ from the reference program's by a relative error of at most 0.025.
Values may be sent and summed in bfloat16 or wider, within the bound.
No kernel may reach another device: no remote copies, remote signals or barrier semaphores. Data moves between devices by JAX's collectives and lax.ppermute only.
A program may use at most 128 MiB of HBM per device.

```python
import jax
import jax.numpy as jnp
from jax import lax

D = 12288
F = 24576
TOKENS = 2048
N_ROW = 8
N_COL = 16


def level_of(key, shape, shards, smallest, largest):
    def one(position, shards_of):
        draws = jax.random.uniform(jax.random.fold_in(jax.random.fold_in(key, 6), position), (shards_of,), jnp.float32, smallest / len(shards), largest / len(shards))
        return jnp.repeat(jnp.exp(draws), shape[position] // shards_of).reshape((-1,) + (1,) * (len(shape) - position - 1))

    loudness = one(*shards[0])
    for cut in shards[1:]:
        loudness = loudness * one(*cut)
    return loudness


def scatter_about(key, shape, scale, reach, split=(), held_as=jnp.bfloat16):
    values = jax.random.normal(key, shape, jnp.float32) * scale
    if len(split) > 0:
        values = level_of(key, shape, split, -0.22, 0.18) * values
    return jnp.clip(values, min=-reach, max=reach).astype(held_as)


def setup_inputs(seed: int = 0) -> dict:
    key_of = jax.random.split(jax.random.key(seed), 4)
    acts = scatter_about(key_of[0], (TOKENS, D), 1.0, 6.0, ((0, 8), (1, 16)))
    weight = scatter_about(key_of[1], (D, F), D ** -0.5, 0.0546875, ((0, 16), (1, 8)))
    cotangent = scatter_about(key_of[2], (TOKENS, F), 0.2, 1.1953125, ((0, 16), (1, 8)))
    return {"acts": acts, "weight": weight, "cotangent": cotangent}


scale_c = 0.7978845608028654
cubic_c = 0.044715


def gelu_value(v):
    inner = jnp.tanh(scale_c * (v + cubic_c * v * v * v))
    return 0.5 * v * (1.0 + inner)


def gelu_slope(v):
    inner = jnp.tanh(scale_c * (v + cubic_c * v * v * v))
    return 0.5 * (1.0 + inner) + 0.5 * v * (1.0 - inner * inner) * scale_c * (1.0 + 3.0 * cubic_c * v * v)


def reference(acts, weight, cotangent):
    width_block = D // N_COL
    unit_block = F // N_ROW

    def add_width(total, index):
        start = (index * width_block).astype(jnp.int32)
        cols = lax.dynamic_slice_in_dim(acts, start, width_block, 1)
        rows = lax.dynamic_slice_in_dim(weight, start, width_block, 0)
        term = jnp.dot(cols, rows, preferred_element_type=jnp.float32).astype(jnp.bfloat16)
        term = lax.optimization_barrier(term)
        return total + term.astype(jnp.float32), None

    pre, unused = lax.scan(add_width, jnp.zeros((TOKENS, F), jnp.float32), jnp.arange(N_COL, dtype=jnp.int32))
    hidden = gelu_value(pre).astype(jnp.bfloat16)
    back = (cotangent.astype(jnp.float32) * gelu_slope(pre)).astype(jnp.bfloat16)

    def add_units(total, index):
        start = (index * unit_block).astype(jnp.int32)
        cols = lax.dynamic_slice_in_dim(back, start, unit_block, 1)
        rows = lax.dynamic_slice_in_dim(weight, start, unit_block, 1)
        term = lax.dot_general(cols, rows, (((1,), (1,)), ((), ())), preferred_element_type=jnp.float32).astype(jnp.bfloat16)
        term = lax.optimization_barrier(term)
        return total + term.astype(jnp.float32), None

    grad_sum, unused = lax.scan(add_units, jnp.zeros((TOKENS, D), jnp.float32), jnp.arange(N_ROW, dtype=jnp.int32))
    grad_acts = grad_sum.astype(jnp.bfloat16)
    grad_weight = lax.dot_general(acts, back, (((0,), (0,)), ((), ())), preferred_element_type=jnp.float32).astype(jnp.bfloat16)
    return hidden, grad_acts, grad_weight
```

```python
import jax
import jax.numpy as jnp
from jax import lax
from jax.sharding import Mesh, PartitionSpec as P

scale_c = 0.7978845608028654
cubic_c = 0.044715
f32, bf16 = jnp.float32, jnp.bfloat16

AXES = (("y", 4), ("zh", 2), ("zl", 2), ("x", 4), ("c", 2))
SIZE = dict(AXES)
CHUNKS = (64, 64)


def gelu_value(v):
    inner = jnp.tanh(scale_c * (v + cubic_c * v * v * v))
    return 0.5 * v * (1.0 + inner)


def gelu_slope(v):
    inner = jnp.tanh(scale_c * (v + cubic_c * v * v * v))
    return 0.5 * (1.0 + inner) + 0.5 * v * (1.0 - inner * inner) * scale_c * (
        1.0 + 3.0 * cubic_c * v * v
    )


def shift(value, axis, step):
    n = SIZE[axis]
    return lax.ppermute(value, axis, [(i, (i + step) % n) for i in range(n)])


def pick(value, index, dim):
    return lax.dynamic_index_in_dim(value, index, dim, keepdims=False)


def paired(own, other, axis, dim):
    first = lax.axis_index(axis) == 0
    return jnp.where(
        first, jnp.concatenate([own, other], dim), jnp.concatenate([other, own], dim)
    )


def exchange4(blocks_of, axis):
    me = lax.axis_index(axis)
    return [shift(blocks_of((me + s) % 4), axis, s) for s in (1, 2, 3)]


def spread4(own, axis, dim):
    me = lax.axis_index(axis)
    got = {s: shift(own, axis, s) for s in (1, 2, 3)}
    rel = [own, got[3], got[2], got[1]]
    both = jnp.stack(rel + rel[:3], dim)
    return lax.dynamic_slice_in_dim(both, (4 - me) % 4, 4, dim)


def per_device(acts, weight, cotangent):
    rows, depth = acts.shape
    units = weight.shape[1]
    half = units // 2
    cut = half // 2
    zl, x, zh, y, c = (lax.axis_index(a) for a in ("zl", "x", "zh", "y", "c"))

    def unit_half(value, which):
        return lax.dynamic_slice_in_dim(value, which * half, half, 1)

    weight_own = unit_half(weight, c)
    weight_two = jnp.concatenate([weight_own, shift(unit_half(weight, 1 - c), "c", 1)], 0)
    cot_two = paired(
        unit_half(cotangent, c)[None], shift(unit_half(cotangent, 1 - c), "c", 1)[None], "c", 0
    )
    acts_two = acts.reshape(2, rows // 2, depth)

    hidden_own, hidden_sib, grads, products = [], [], [], None
    start = 0
    starts = []
    for size in CHUNKS:
        starts.append(start)
        start += size

    def gather_acts(j):
        size = CHUNKS[j]
        n = 2 * size
        own = acts_two[:, starts[j] : starts[j] + size].reshape(n, depth)
        pair = paired(own[None], shift(own, "zh", 1)[None], "zh", 0)
        mine = spread4(pair, "y", 0).reshape(8 * n, depth)
        return jnp.concatenate([mine, shift(mine, "c", 1)], 1)

    def project(a):
        return jnp.dot(a, weight_two, preferred_element_type=f32).astype(bf16)

    def sum_terms(p, n):
        p = p.reshape(2, 4, n, half)
        pa, pb = p[..., :cut], p[..., cut:]
        ra = exchange4(lambda k: pick(pa, k, 1), "x")
        rb = shift(pick(pb, 1 - zl, 0), "zl", 1)
        sa = pick(pa, x, 1).astype(f32) + ra[0] + ra[1] + ra[2]
        sb = pick(pb, zl, 0).astype(f32) + rb
        sb16 = sb.astype(bf16)
        qa = shift(pick(sa, 1 - zl, 0).astype(bf16), "zl", 1)
        qb = exchange4(lambda k: pick(sb16, k, 0), "x")
        pre_a = pick(sa, zl, 0) + qa
        pre_b = pick(sb, x, 0) + qb[0] + qb[1] + qb[2]
        return pre_a, pre_b

    def gather_back(ba, bb, n):
        pair = paired(ba[None], shift(ba, "zl", 1)[None], "zl", 0)
        four = spread4(bb, "x", 0)
        full_a = spread4(pair, "x", 1)
        full_b = paired(four[None], shift(four, "zl", 1)[None], "zl", 0)
        return jnp.concatenate([full_a, full_b], 3).reshape(8 * n, half)

    def sum_grads(g, n):
        mine = g[:, :depth].astype(f32) + shift(g[:, depth:], "c", 1)
        mine = mine.astype(bf16).reshape(4, 2, n, depth)
        got = exchange4(lambda k: pick(mine, k, 0), "y")
        part = pick(mine, y, 0).astype(f32) + got[0] + got[1] + got[2]
        other = shift(pick(part, 1 - zh, 0).astype(bf16), "zh", 1)
        return (pick(part, zh, 0) + other).astype(bf16)

    for j, size in enumerate(CHUNKS):
        n = 2 * size
        a = gather_acts(j)
        pre = sum_terms(project(a), n)
        cot = cot_two[:, starts[j] : starts[j] + size].reshape(n, half)
        hid = [gelu_value(v).astype(bf16) for v in pre]
        back = [
            (cot[:, k * cut : (k + 1) * cut].astype(f32) * gelu_slope(v)).astype(bf16)
            for k, v in enumerate(pre)
        ]
        hid = jnp.concatenate(hid, 1).reshape(2, size, half)
        hidden_own.append(pick(hid, c, 0))
        hidden_sib.append(pick(hid, 1 - c, 0))
        full = gather_back(*back, n)
        g = lax.dot_general(
            full, weight_two, (((1,), (1,)), ((), ())), preferred_element_type=f32
        ).astype(bf16)
        grads.append(sum_grads(g, n).reshape(2, size, depth))
        product = lax.dot_general(
            a, full, (((0,), (0,)), ((), ())), preferred_element_type=f32
        )
        products = product if products is None else products + product

    hid_own = jnp.concatenate(hidden_own, 0)
    hid_other = shift(jnp.concatenate(hidden_sib, 0), "c", 1)
    hidden = paired(hid_own, hid_other, "c", 1)
    grad_acts = jnp.concatenate(grads, 1).reshape(rows, depth)
    w16 = products.astype(bf16)
    grad_weight = paired(w16[:depth], shift(w16[depth:], "c", 1), "c", 1)
    return hidden, grad_acts, grad_weight


def solution(mesh):
    fine = Mesh(mesh.devices.reshape([n for _, n in AXES]), [a for a, _ in AXES])
    row, col = ("y", "zh"), ("zl", "x", "c")
    return jax.shard_map(
        per_device,
        mesh=fine,
        in_specs=(P(row, col), P(col, row), P(col, row)),
        out_specs=(P(col, row), P(row, col), P(col, row)),
        check_vma=False,
    )
```

```python
import jax
import jax.numpy as jnp
from jax import lax
from jax.experimental.layout import Layout, with_layout_constraint
from jax.sharding import Mesh, PartitionSpec as P

scale_c = 0.7978845608028654
cubic_c = 0.044715
f32, bf16 = jnp.float32, jnp.bfloat16

AXES = (("y", 4), ("zh", 2), ("zl", 2), ("x", 4), ("c", 2))
SIZE = dict(AXES)
CHUNKS = (128,)
CUT = 768
DEPTH_CUT = 384


def gelu_value(v):
    inner = jnp.tanh(scale_c * (v + cubic_c * v * v * v))
    return 0.5 * v * (1.0 + inner)


def gelu_slope(v):
    inner = jnp.tanh(scale_c * (v + cubic_c * v * v * v))
    return 0.5 * (1.0 + inner) + 0.5 * v * (1.0 - inner * inner) * scale_c * (
        1.0 + 3.0 * cubic_c * v * v
    )


def after(value, token):
    return value if token is None else lax.optimization_barrier((value, token))[0]


def shift(value, axis, step):
    n = SIZE[axis]
    return lax.ppermute(value, axis, [(i, (i + step) % n) for i in range(n)])


def pick(value, index, dim):
    return lax.dynamic_index_in_dim(value, index, dim, keepdims=False)


def put(buffer, value, index, dim):
    return lax.dynamic_update_index_in_dim(buffer, value, index, dim)


def send4(block_of, axis, token=None):
    me = lax.axis_index(axis)
    n = SIZE[axis]
    return {s: shift(after(block_of((me + s) % n), token), axis, s) for s in (1, 3, 2)}


def spread4(own, axis, token=None):
    me = lax.axis_index(axis)
    own = after(own, token)
    got = [((me + 4 - s) % 4, shift(own, axis, s)) for s in (1, 3, 2)]
    return [(me, own)] + got


def swap(value, axis, token=None):
    return shift(after(value, token), axis, 1)


def total_of(own, got):
    return own.astype(f32) + got[1] + got[3] + got[2]


def per_device(acts, weight, cotangent):
    rows, depth = acts.shape
    half = weight.shape[1] // 2
    cut, dcut = min(CUT, half // 2), min(DEPTH_CUT, depth // 2)
    zl, x, zh, y, c = (lax.axis_index(a) for a in ("zl", "x", "zh", "y", "c"))
    dot = lambda a, b, dims: lax.dot_general(a, b, (dims, ((), ())), preferred_element_type=f32)

    def unit_half(value, which):
        return lax.dynamic_slice_in_dim(value, which * half, half, 1)

    acts_two = acts.reshape(2, rows // 2, depth)
    starts = [sum(CHUNKS[:j]) for j in range(len(CHUNKS))]

    def gather_acts(j):
        size = CHUNKS[j]
        n = 2 * size
        own = acts_two[:, starts[j] : starts[j] + size].reshape(n, depth)
        mine = jnp.zeros((4, 2, n, depth), bf16)
        pa, pb = own[:, :dcut], own[:, dcut:]
        other = swap(pb, "zh")
        four = jnp.zeros((4, n, dcut), bf16)
        for place, block in spread4(pa, "y"):
            four = put(four, block, place, 0)
        pair = put(put(jnp.zeros((2, n, depth - dcut), bf16), pb, zh, 0), other, 1 - zh, 0)
        four_other = swap(four, "zh")
        for place, block in spread4(pair, "y"):
            mine = lax.dynamic_update_slice(mine, block[None], (place, 0, 0, dcut))
        mine = lax.dynamic_update_slice(mine, four[:, None], (0, zh, 0, 0))
        mine = lax.dynamic_update_slice(mine, four_other[:, None], (0, 1 - zh, 0, 0))
        mine = mine.reshape(8 * n, depth)
        return mine, swap(mine, "c")

    def sum_grads(mine, n):
        pa, pb = mine[..., :dcut], mine[..., dcut:]
        gb = swap(pick(pb, 1 - zh, 1), "zh")
        ga = send4(lambda k: pick(pa, k, 0), "y")
        sb = pick(pb, zh, 1).astype(f32) + gb
        sa = total_of(pick(pa, y, 0), ga)
        sb16 = sb.astype(bf16)
        qa = swap(pick(sa, 1 - zh, 0).astype(bf16), "zh")
        qb = send4(lambda k: pick(sb16, k, 0), "y")
        ra = pick(sa, zh, 0) + qa
        rb = total_of(pick(sb, y, 0), qb)
        return jnp.concatenate([ra.astype(bf16), rb.astype(bf16)], 1)

    weight_own = unit_half(weight, c)
    weight_sib = swap(unit_half(weight, 1 - c), "c")
    cot_two = jnp.zeros((2, rows // 2, half), bf16)
    cot_two = put(cot_two, unit_half(cotangent, c), c, 0)
    cot_two = put(cot_two, swap(unit_half(cotangent, 1 - c), "c"), 1 - c, 0)

    own_acts, sib_acts = zip(*[gather_acts(j) for j in range(len(CHUNKS))])
    hidden_own, hidden_sib, full = [], [], []
    xt = zt = None
    for j, size in enumerate(CHUNKS):
        n = 2 * size
        ao, ab = own_acts[j], sib_acts[j]

        def project(low, high):
            v = dot(ao, weight_own[:, low:high], ((1,), (0,)))
            v = v + dot(ab, weight_sib[:, low:high], ((1,), (0,)))
            return v.astype(bf16).reshape(2, 4, n, high - low)

        pb = project(cut, half)
        gb = swap(pick(pb, 1 - zl, 0), "zl", zt)
        pa = project(0, cut)
        ga = send4(lambda k: pick(pa, k, 1), "x", xt)
        sb = pick(pb, zl, 0).astype(f32) + gb
        sb16 = sb.astype(bf16)
        sa = total_of(pick(pa, x, 1), ga)
        qb = send4(lambda k: pick(sb16, k, 0), "x")
        qa = swap(pick(sa, 1 - zl, 0).astype(bf16), "zl")
        pre_a = pick(sa, zl, 0) + qa
        pre_b = total_of(pick(sb, x, 0), qb)

        cot = cot_two[:, starts[j] : starts[j] + size].reshape(n, half)
        ba = (cot[:, :cut].astype(f32) * gelu_slope(pre_a)).astype(bf16)
        bb = (cot[:, cut:].astype(f32) * gelu_slope(pre_b)).astype(bf16)
        hid = jnp.concatenate([gelu_value(pre_a), gelu_value(pre_b)], 1).astype(bf16)
        hid = hid.reshape(2, size, half)
        hidden_own.append(pick(hid, c, 0))
        hidden_sib.append(pick(hid, 1 - c, 0))

        ra = swap(ba, "zl")
        four = jnp.zeros((4, n, half - cut), bf16)
        for place, block in spread4(bb, "x"):
            four = put(four, block, place, 0)
        pair = put(put(jnp.zeros((2, n, cut), bf16), ba, zl, 0), ra, 1 - zl, 0)
        other = swap(four, "zl")
        fa = jnp.zeros((2, 4, n, cut), bf16)
        for place, block in spread4(pair, "x"):
            fa = put(fa, block, place, 1)
        fb = put(put(jnp.zeros((2, 4, n, half - cut), bf16), four, zl, 0), other, 1 - zl, 0)
        full.append((fa.reshape(8 * n, cut), fb.reshape(8 * n, half - cut)))

    grads = []
    prod = {}
    for j, size in enumerate(CHUNKS):
        n = 2 * size
        fa, fb = full[j]

        def back_to(w):
            v = dot(fa, w[:, :cut], ((1,), (1,))) + dot(fb, w[:, cut:], ((1,), (1,)))
            return v

        for_sib = swap(back_to(weight_sib).astype(bf16), "c")
        mine = (back_to(weight_own) + for_sib).astype(bf16).reshape(4, 2, n, depth)
        grads.append(sum_grads(mine, n).reshape(2, size, depth))
        for name, v, f in (
            ("sa", sib_acts[j], fa),
            ("sb", sib_acts[j], fb),
            ("oa", own_acts[j], fa),
            ("ob", own_acts[j], fb),
        ):
            r = dot(v, f, ((0,), (0,)))
            prod[name] = prod[name] + r if name in prod else r

    hid_other = swap(jnp.concatenate(hidden_sib, 0), "c")
    hidden = jnp.zeros(cotangent.shape, bf16)
    hidden = lax.dynamic_update_slice_in_dim(hidden, jnp.concatenate(hidden_own, 0), c * half, 1)
    hidden = lax.dynamic_update_slice_in_dim(hidden, hid_other, (1 - c) * half, 1)
    grad_acts = jnp.concatenate(grads, 1).reshape(rows, depth)
    row_major = lambda v: with_layout_constraint(v.astype(bf16), Layout((0, 1)))
    grad_weight = jnp.zeros(weight.shape, bf16)
    for low, o, s in ((0, "oa", "sa"), (cut, "ob", "sb")):
        got = swap(row_major(prod[s]), "c")
        grad_weight = lax.dynamic_update_slice_in_dim(
            grad_weight, row_major(prod[o]), c * half + low, 1
        )
        grad_weight = lax.dynamic_update_slice_in_dim(grad_weight, got, (1 - c) * half + low, 1)
    return hidden, grad_acts, grad_weight


def solution(mesh):
    fine = Mesh(mesh.devices.reshape([n for _, n in AXES]), [a for a, _ in AXES])
    row, col = ("y", "zh"), ("zl", "x", "c")
    return jax.shard_map(
        per_device,
        mesh=fine,
        in_specs=(P(row, col), P(col, row), P(col, row)),
        out_specs=(P(col, row), P(row, col), P(col, row)),
        check_vma=False,
    )
```

```python
import math

import jax
import jax.numpy as jnp
from jax import lax
from jax.experimental import pallas as pl
from jax.experimental.layout import Layout, with_layout_constraint
from jax.experimental.pallas import tpu as pltpu
from jax.sharding import Mesh, PartitionSpec as P

scale_c = 0.7978845608028654
cubic_c = 0.044715
f32, bf16 = jnp.float32, jnp.bfloat16

AXES = (("y", 4), ("zh", 2), ("zl", 2), ("x", 4), ("c", 2))
SIZE = dict(AXES)
CHUNKS = (128,)
CUT = 768
VMEM = 16 * 2**20
NN, NT, TN = ((1,), (0,)), ((1,), (1,)), ((0,), (0,))
DEPTH_CUT = 384


def gelu_value(v):
    inner = jnp.tanh(scale_c * (v + cubic_c * v * v * v))
    return 0.5 * v * (1.0 + inner)


def gelu_slope(v):
    inner = jnp.tanh(scale_c * (v + cubic_c * v * v * v))
    return 0.5 * (1.0 + inner) + 0.5 * v * (1.0 - inner * inner) * scale_c * (
        1.0 + 3.0 * cubic_c * v * v
    )


def after(value, token):
    return value if token is None else lax.optimization_barrier((value, token))[0]


def shift(value, axis, step):
    n = SIZE[axis]
    return lax.ppermute(value, axis, [(i, (i + step) % n) for i in range(n)])


def pick(value, index, dim):
    return lax.dynamic_index_in_dim(value, index, dim, keepdims=False)


def put(buffer, value, index, dim):
    return lax.dynamic_update_index_in_dim(buffer, value, index, dim)


def send4(block_of, axis, token=None):
    me = lax.axis_index(axis)
    n = SIZE[axis]
    return {s: shift(after(block_of((me + s) % n), token), axis, s) for s in (1, 3, 2)}


def spread4(own, axis, token=None):
    me = lax.axis_index(axis)
    own = after(own, token)
    got = [((me + 4 - s) % 4, shift(own, axis, s)) for s in (1, 3, 2)]
    return [(me, own)] + got


def ring_sum4(block_of, axis):
    me = lax.axis_index(axis)
    far = block_of((me + 2) % 4)
    up, down = shift(far[0], axis, 1), shift(far[1], axis, 3)
    above, below = block_of((me + 1) % 4), block_of((me + 3) % 4)
    above = jnp.stack([(above[0].astype(f32) + up).astype(bf16), above[1]])
    below = jnp.stack([below[0], (below[1].astype(f32) + down).astype(bf16)])
    return block_of(me).astype(f32) + shift(above, axis, 1) + shift(below, axis, 3)


def swap(value, axis, token=None):
    return shift(after(value, token), axis, 1)


def total_of(own, got):
    return own.astype(f32) + got[1] + got[3] + got[2]


def call(kernel, out, grid, ins, specs, out_spec, flops, prefetch=None, aliases={}):
    scalars = () if prefetch is None else (prefetch,)
    moved = sum(v.size * v.dtype.itemsize for v in ins if v is not None)
    return pl.pallas_call(
        kernel,
        out_shape=jax.ShapeDtypeStruct(out, bf16),
        grid_spec=pltpu.PrefetchScalarGridSpec(
            num_scalar_prefetch=len(scalars),
            grid=grid,
            in_specs=specs,
            out_specs=out_spec,
        ),
        compiler_params=pltpu.CompilerParams(vmem_limit_bytes=VMEM),
        cost_estimate=pl.CostEstimate(flops=flops, bytes_accessed=moved, transcendentals=0),
        input_output_aliases=aliases,
    )(*scalars, *ins)


def row_major(value):
    return with_layout_constraint(value, Layout(tuple(range(value.ndim))))


def dot(a, b, dims):
    return lax.dot_general(a, b, (dims, ((), ())), preferred_element_type=f32)


def project(own, sib, weight, weight_sib, c, part, cut):
    rows, depth = own.shape
    m = math.gcd(rows, 512)

    def kernel(c_ref, a_ref, b_ref, w_ref, v_ref, o_ref):
        total = dot(a_ref[...], w_ref[...], NN) + dot(b_ref[...], v_ref[...], NN)
        o_ref[...] = total.astype(bf16)

    return call(
        kernel,
        (rows, cut),
        (rows // m,),
        (own, sib, weight, weight_sib),
        [
            pl.BlockSpec((m, depth), lambda i, c: (i, 0)),
            pl.BlockSpec((m, depth), lambda i, c: (i, 0)),
            pl.BlockSpec((depth, cut), lambda i, c: (0, part)),
            pl.BlockSpec((depth, cut), lambda i, c: (0, part)),
        ],
        pl.BlockSpec((m, cut), lambda i, c: (i, 0)),
        4 * rows * depth * cut,
        c,
    )


def back_to(fa, fb, weight, column, first, rows, add=None):
    cut = fa.shape[1]
    depth = weight.shape[0]
    m = math.gcd(rows, 512)
    base = first // m

    def kernel(c_ref, a_ref, b_ref, w_ref, *refs):
        total = dot(a_ref[...], w_ref[:, :cut], NT) + dot(b_ref[...], w_ref[:, cut:], NT)
        if add is not None:
            total = total + refs[0][...]
        refs[-1][...] = total.astype(bf16)

    specs = [
        pl.BlockSpec((m, cut), lambda i, c: (i + base, 0)),
        pl.BlockSpec((m, cut), lambda i, c: (i + base, 0)),
        pl.BlockSpec((depth, 2 * cut), lambda i, c: (0, c[0])),
    ]
    ins = (fa, fb, weight)
    if add is not None:
        specs.append(pl.BlockSpec((m, depth), lambda i, c: (i, 0)))
        ins = ins + (add,)
    return call(
        kernel,
        (rows, depth),
        (rows // m,),
        ins,
        specs,
        pl.BlockSpec((m, depth), lambda i, c: (i, 0)),
        4 * rows * depth * cut,
        column,
    )


def per_device(acts, weight, cotangent):
    rows, depth = acts.shape
    half = weight.shape[1] // 2
    cut, dcut = min(CUT, half // 2), min(DEPTH_CUT, depth // 2)
    zl, x, zh, y, c = (lax.axis_index(a) for a in ("zl", "x", "zh", "y", "c"))

    def unit_half(value, which):
        return lax.dynamic_slice_in_dim(value, which * half, half, 1)

    acts_two = acts.reshape(2, rows // 2, depth)
    starts = [sum(CHUNKS[:j]) for j in range(len(CHUNKS))]

    zero = jnp.zeros((1,), jnp.int32)
    weight_own = unit_half(weight, c)
    weight_sib = swap(unit_half(weight, 1 - c), "c")

    def gather_acts(j):
        size = CHUNKS[j]
        n = 2 * size
        own = acts_two[:, starts[j] : starts[j] + size].reshape(n, depth)
        mine = jnp.zeros((4, 2, n, depth), bf16)
        pa, pb = own[:, :dcut], own[:, dcut:]
        other = swap(pb, "zh")
        four = jnp.zeros((4, n, dcut), bf16)
        for place, block in spread4(pa, "y"):
            four = put(four, block, place, 0)
        pair = put(put(jnp.zeros((2, n, depth - dcut), bf16), pb, zh, 0), other, 1 - zh, 0)
        four, pair = after((four, pair), (weight_own, weight_sib))
        four_other = swap(four, "zh")
        for place, block in spread4(pair, "y"):
            mine = lax.dynamic_update_slice(mine, block[None], (place, 0, 0, dcut))
        mine = lax.dynamic_update_slice(mine, four[:, None], (0, zh, 0, 0))
        mine = lax.dynamic_update_slice(mine, four_other[:, None], (0, 1 - zh, 0, 0))
        mine = row_major(mine.reshape(8 * n, depth))
        return mine, row_major(swap(mine, "c"))

    def sum_grads(mine, n, beside):
        pa, pb = mine[..., :dcut], mine[..., dcut:]
        gb = swap(pick(pb, 1 - zh, 1), "zh")
        ga = send4(lambda k: pick(pa, k, 0), "y")
        sb = pick(pb, zh, 1).astype(f32) + gb
        sa = total_of(pick(pa, y, 0), ga)
        sa, sb, beside = lax.optimization_barrier((sa, sb, beside))
        sb16 = sb.astype(bf16)
        qa = swap(pick(sa, 1 - zh, 0).astype(bf16), "zh")
        qb = send4(lambda k: pick(sb16, k, 0), "y")
        ra = pick(sa, zh, 0) + qa
        rb = total_of(pick(sb, y, 0), qb)
        return jnp.concatenate([ra.astype(bf16), rb.astype(bf16)], 1), beside

    cot_two = jnp.zeros((2, rows // 2, half), bf16)
    cot_two = put(cot_two, unit_half(cotangent, c), c, 0)
    cot_two = put(cot_two, swap(unit_half(cotangent, 1 - c), "c"), 1 - c, 0)

    own_acts, sib_acts = zip(*[gather_acts(j) for j in range(len(CHUNKS))])
    hidden_own, hidden_sib, full = [], [], []
    xt = zt = None
    for j, size in enumerate(CHUNKS):
        n = 2 * size
        ao, ab = own_acts[j], sib_acts[j]

        pb = project(ao, ab, weight_own, weight_sib, zero, 1, cut).reshape(2, 4, n, cut)
        gb = swap(pick(pb, 1 - zl, 0), "zl", zt)
        pa = project(ao, ab, weight_own, weight_sib, zero, 0, cut).reshape(2, 4, n, cut)
        sb = pick(pb, zl, 0).astype(f32) + gb
        sb16 = sb.astype(bf16)
        sa = ring_sum4(lambda k: pick(pa, k, 1), "x")
        qb = send4(lambda k: pick(sb16, k, 0), "x")
        qa = swap(pick(sa, 1 - zl, 0).astype(bf16), "zl")
        pre_a = pick(sa, zl, 0) + qa
        pre_b = total_of(pick(sb, x, 0), qb)

        cot = cot_two[:, starts[j] : starts[j] + size].reshape(n, half)
        ba = (cot[:, :cut].astype(f32) * gelu_slope(pre_a)).astype(bf16)
        bb = (cot[:, cut:].astype(f32) * gelu_slope(pre_b)).astype(bf16)
        hid = jnp.concatenate([gelu_value(pre_a), gelu_value(pre_b)], 1).astype(bf16)
        hid = hid.reshape(2, size, half)
        hidden_own.append(pick(hid, c, 0))
        hidden_sib.append(pick(hid, 1 - c, 0))

        ra = swap(ba, "zl")
        four = jnp.zeros((4, n, half - cut), bf16)
        for place, block in spread4(bb, "x"):
            four = put(four, block, place, 0)
        pair = put(put(jnp.zeros((2, n, cut), bf16), ba, zl, 0), ra, 1 - zl, 0)
        other = swap(four, "zl")
        fa = jnp.zeros((2, 4, n, cut), bf16)
        low, high = shift(pair, "x", 1), shift(pair, "x", 3)
        far0, far1 = shift(low[0], "x", 1), shift(high[1], "x", 3)
        for place, block in ((x, pair), ((x + 3) % 4, low), ((x + 1) % 4, high)):
            fa = put(fa, block, place, 1)
        for k, block in enumerate((far0, far1)):
            fa = lax.dynamic_update_slice(fa, block[None, None], (k, (x + 2) % 4, 0, 0))
        fb = put(put(jnp.zeros((2, 4, n, half - cut), bf16), four, zl, 0), other, 1 - zl, 0)
        full.append((fa.reshape(8 * n, cut), fb.reshape(8 * n, half - cut)))

    hid_other = swap(jnp.concatenate(hidden_sib, 0), "c")
    hidden = jnp.zeros(cotangent.shape, bf16)
    hidden = lax.dynamic_update_slice_in_dim(hidden, jnp.concatenate(hidden_own, 0), c * half, 1)
    hidden = lax.dynamic_update_slice_in_dim(hidden, hid_other, (1 - c) * half, 1)

    fa, fb = after(full[0], hid_other)
    n = 2 * CHUNKS[0]
    zero = jnp.zeros((1,), jnp.int32)
    mid = 4 * n
    sent = [swap(back_to(fa, fb, weight_sib, zero, k * mid, mid), "c") for k in range(2)]
    parts = [back_to(fa, fb, weight_own, zero, k * mid, mid, sent[k]) for k in range(2)]
    mine = jnp.concatenate(parts, 0).reshape(4, 2, n, depth)
    fa, fb = after((fa, fb), mine)
    grad_weight = jnp.zeros(weight.shape, bf16)
    product = lambda v, f: row_major(dot(v, f, TN).astype(bf16))
    got = [swap(product(sib_acts[0], f), "c") for f in (fa, fb)]
    grad_weight = lax.dynamic_update_slice_in_dim(
        grad_weight, product(own_acts[0], fa), c * half, 1
    )
    grad_acts, grad_weight = sum_grads(mine, n, grad_weight)
    grad_weight = lax.dynamic_update_slice_in_dim(
        grad_weight, product(own_acts[0], fb), c * half + cut, 1
    )
    for low, v in ((0, got[0]), (cut, got[1])):
        grad_weight = lax.dynamic_update_slice_in_dim(grad_weight, v, (1 - c) * half + low, 1)
    return hidden, grad_acts, grad_weight


def solution(mesh):
    fine = Mesh(mesh.devices.reshape([n for _, n in AXES]), [a for a, _ in AXES])
    row, col = ("y", "zh"), ("zl", "x", "c")
    return jax.shard_map(
        per_device,
        mesh=fine,
        in_specs=(P(row, col), P(col, row), P(col, row)),
        out_specs=(P(col, row), P(row, col), P(col, row)),
        check_vma=False,
    )
```

```python
import math

import jax
import jax.numpy as jnp
from jax import lax
from jax.experimental import pallas as pl
from jax.experimental.layout import Layout, with_layout_constraint
from jax.experimental.pallas import tpu as pltpu
from jax.sharding import Mesh, PartitionSpec as P

scale_c = 0.7978845608028654
cubic_c = 0.044715
f32, bf16 = jnp.float32, jnp.bfloat16

AXES = (("y", 4), ("zh", 2), ("zl", 2), ("x", 4), ("c", 2))
SIZE = dict(AXES)
CHUNKS = (128,)
CUT = 768
VMEM = 12 * 2**20
TILE = 2048
NN, NT, TN = ((1,), (0,)), ((1,), (1,)), ((0,), (0,))
DEPTH_CUT = 384


def gelu_value(v):
    inner = jnp.tanh(scale_c * (v + cubic_c * v * v * v))
    return 0.5 * v * (1.0 + inner)


def gelu_slope(v):
    inner = jnp.tanh(scale_c * (v + cubic_c * v * v * v))
    return 0.5 * (1.0 + inner) + 0.5 * v * (1.0 - inner * inner) * scale_c * (
        1.0 + 3.0 * cubic_c * v * v
    )


def after(value, token):
    return value if token is None else lax.optimization_barrier((value, token))[0]


def shift(value, axis, step):
    n = SIZE[axis]
    return lax.ppermute(value, axis, [(i, (i + step) % n) for i in range(n)])


def pick(value, index, dim):
    return lax.dynamic_index_in_dim(value, index, dim, keepdims=False)


def put(buffer, value, index, dim):
    return lax.dynamic_update_index_in_dim(buffer, value, index, dim)


def send4(block_of, axis, token=None):
    me = lax.axis_index(axis)
    n = SIZE[axis]
    return {s: shift(after(block_of((me + s) % n), token), axis, s) for s in (1, 3, 2)}


def spread4(own, axis, token=None):
    me = lax.axis_index(axis)
    own = after(own, token)
    got = [((me + 4 - s) % 4, shift(own, axis, s)) for s in (1, 3, 2)]
    return [(me, own)] + got


def ring_sum4(block_of, axis):
    me = lax.axis_index(axis)
    far = block_of((me + 2) % 4)
    up, down = shift(far[0], axis, 1), shift(far[1], axis, 3)
    above, below = block_of((me + 1) % 4), block_of((me + 3) % 4)
    above = jnp.stack([(above[0].astype(f32) + up).astype(bf16), above[1]])
    below = jnp.stack([below[0], (below[1].astype(f32) + down).astype(bf16)])
    return block_of(me).astype(f32) + shift(above, axis, 1) + shift(below, axis, 3)


def swap(value, axis, token=None):
    return shift(after(value, token), axis, 1)


def total_of(own, got):
    return own.astype(f32) + got[1] + got[3] + got[2]


def call(kernel, out, ins, flops):
    whole = pl.BlockSpec(memory_space=pltpu.VMEM)
    moved = sum(v.size * v.dtype.itemsize for v in ins)
    return pl.pallas_call(
        kernel,
        out_shape=jax.ShapeDtypeStruct(out, bf16),
        in_specs=[whole] * len(ins),
        out_specs=whole,
        compiler_params=pltpu.CompilerParams(vmem_limit_bytes=VMEM),
        cost_estimate=pl.CostEstimate(flops=flops, bytes_accessed=moved, transcendentals=0),
    )(*ins)


def row_major(value):
    return with_layout_constraint(value, Layout(tuple(range(value.ndim))))


def dot(a, b, dims):
    return lax.dot_general(a, b, (dims, ((), ())), preferred_element_type=f32)


def project(own, sib, weight, weight_sib, low, high):
    rows, depth = own.shape
    m = math.gcd(rows, TILE)

    def kernel(a_ref, b_ref, w_ref, v_ref, o_ref):
        def step(i, carry):
            at = pl.ds(pl.multiple_of(i * m, m), m)
            total = dot(a_ref[at], w_ref[:, low:high], NN) + dot(b_ref[at], v_ref[:, low:high], NN)
            o_ref[at] = total.astype(bf16)
            return carry

        lax.fori_loop(0, rows // m, step, 0)

    flops = 4 * rows * depth * (high - low)
    return call(kernel, (rows, high - low), (own, sib, weight, weight_sib), flops)


def back_to(fa, fb, weight, part, add=None):
    blocks, rows, cut = fa.shape
    depth = weight.shape[0]
    rows = rows // 2
    group = max(1, min(blocks, TILE // rows))

    def kernel(a_ref, b_ref, w_ref, *refs):
        def step(i, carry):
            at = pl.ds(i * group, group)
            here = pl.ds(part * rows, rows)
            a = a_ref[at, here].reshape(group * rows, cut)
            b = b_ref[at, here].reshape(group * rows, fb.shape[2])
            total = dot(a, w_ref[:, :cut], NT) + dot(b, w_ref[:, cut:], NT)
            if add is not None:
                total = total + refs[0][at].reshape(group * rows, depth)
            refs[-1][at] = total.astype(bf16).reshape(group, rows, depth)
            return carry

        lax.fori_loop(0, blocks // group, step, 0)

    ins = (fa, fb, weight) if add is None else (fa, fb, weight, add)
    return call(kernel, (blocks, rows, depth), ins, 2 * blocks * rows * depth * weight.shape[1])


def weight_product(acts, fa, fb):
    depth, cut = acts.shape[1], fa.shape[1]

    def kernel(t_ref, a_ref, b_ref, o_ref):
        o_ref[:, :cut] = dot(t_ref[...], a_ref[...], TN).astype(bf16)
        o_ref[:, cut:] = dot(t_ref[...], b_ref[...], TN).astype(bf16)

    width = cut + fb.shape[1]
    return call(kernel, (depth, width), (acts, fa, fb), 2 * acts.size * width)


def per_device(acts, weight, cotangent):
    rows, depth = acts.shape
    half = weight.shape[1] // 2
    cut, dcut = CUT, DEPTH_CUT
    zl, x, zh, y, c = (lax.axis_index(a) for a in ("zl", "x", "zh", "y", "c"))

    def unit_half(value, which):
        return lax.dynamic_slice_in_dim(value, which * half, half, 1)

    acts_two = acts.reshape(2, rows // 2, depth)
    starts = [sum(CHUNKS[:j]) for j in range(len(CHUNKS))]

    weight_sib = swap(unit_half(weight, 1 - c), "c")

    def gather_acts(j):
        size = CHUNKS[j]
        n = 2 * size
        own = acts_two[:, starts[j] : starts[j] + size].reshape(n, depth)
        mine = jnp.zeros((4, 2, n, depth), bf16)
        pa, pb = own[:, :dcut], own[:, dcut:]
        other = swap(pb, "zh")
        weight_own = unit_half(after(weight, other), c)
        four = jnp.zeros((4, n, dcut), bf16)
        for place, block in spread4(pa, "y"):
            four = put(four, block, place, 0)
        pair = put(put(jnp.zeros((2, n, depth - dcut), bf16), pb, zh, 0), other, 1 - zh, 0)
        four, pair = after((four, pair), weight_sib)
        four_other = swap(four, "zh")
        for place, block in spread4(pair, "y"):
            mine = lax.dynamic_update_slice(mine, block[None], (place, 0, 0, dcut))
        mine = lax.dynamic_update_slice(mine, four[:, None], (0, zh, 0, 0))
        mine = lax.dynamic_update_slice(mine, four_other[:, None], (0, 1 - zh, 0, 0))
        mine = row_major(mine.reshape(8 * n, depth))
        return mine, row_major(swap(mine, "c")), weight_own

    cot_two = jnp.zeros((2, rows // 2, half), bf16)
    cot_two = put(cot_two, unit_half(cotangent, c), c, 0)
    cot_two = put(cot_two, swap(unit_half(cotangent, 1 - c), "c"), 1 - c, 0)

    ao, ab, weight_own = gather_acts(0)
    hidden_own, hidden_sib, full = [], [], []
    xt = zt = None
    for j, size in enumerate(CHUNKS):
        n = 2 * size

        pb = project(ao, ab, weight_own, weight_sib, cut, half).reshape(2, 4, n, half - cut)
        gb = swap(pick(pb, 1 - zl, 0), "zl", zt)
        pa = project(ao, ab, weight_own, weight_sib, 0, cut).reshape(2, 4, n, cut)
        sb = pick(pb, zl, 0).astype(f32) + gb
        sb16 = sb.astype(bf16)
        sa = ring_sum4(lambda k: pick(pa, k, 1), "x")
        qb = send4(lambda k: pick(sb16, k, 0), "x")
        qa = swap(pick(sa, 1 - zl, 0).astype(bf16), "zl")
        pre_a = pick(sa, zl, 0) + qa
        pre_b = total_of(pick(sb, x, 0), qb)

        cot = cot_two[:, starts[j] : starts[j] + size].reshape(n, half)
        ba = (cot[:, :cut].astype(f32) * gelu_slope(pre_a)).astype(bf16)
        bb = (cot[:, cut:].astype(f32) * gelu_slope(pre_b)).astype(bf16)
        hid = jnp.concatenate([gelu_value(pre_a), gelu_value(pre_b)], 1).astype(bf16)
        hid = hid.reshape(2, size, half)
        hidden_own.append(pick(hid, c, 0))
        hidden_sib.append(pick(hid, 1 - c, 0))

        ra = swap(ba, "zl")
        pieces = spread4(bb, "x")
        first = swap(bb, "zl")
        rest = swap(jnp.stack([v for _, v in pieces[1:]]), "zl")
        fb = jnp.zeros((2, 4, n, half - cut), bf16)
        for k, (place, block) in enumerate(pieces):
            fb = lax.dynamic_update_slice(fb, block[None, None], (zl, place, 0, 0))
            got = first if k == 0 else rest[k - 1]
            fb = lax.dynamic_update_slice(fb, got[None, None], (1 - zl, place, 0, 0))
        pair = put(put(jnp.zeros((2, n, cut), bf16), ba, zl, 0), ra, 1 - zl, 0)
        fa = jnp.zeros((2, 4, n, cut), bf16)
        low, high = shift(pair, "x", 1), shift(pair, "x", 3)
        far0, far1 = shift(low[0], "x", 1), shift(high[1], "x", 3)
        for place, block in ((x, pair), ((x + 3) % 4, low), ((x + 1) % 4, high)):
            fa = put(fa, block, place, 1)
        for k, block in enumerate((far0, far1)):
            fa = lax.dynamic_update_slice(fa, block[None, None], (k, (x + 2) % 4, 0, 0))
        full.append((fa.reshape(8 * n, cut), fb.reshape(8 * n, half - cut)))

    hid_other = swap(jnp.concatenate(hidden_sib, 0), "c")
    hidden = jnp.zeros(cotangent.shape, bf16)
    hidden = lax.dynamic_update_slice_in_dim(hidden, jnp.concatenate(hidden_own, 0), c * half, 1)
    hidden = lax.dynamic_update_slice_in_dim(hidden, hid_other, (1 - c) * half, 1)

    fa, fb = after(full[0], hid_other)
    n = 2 * CHUNKS[0]
    shaped = [v.reshape(8, n, -1) for v in (fa, fb)]
    other_a = swap(fa, "c")
    sent = [swap(back_to(*shaped, weight_sib, h), "c") for h in range(2)]
    parts = []
    for h in range(2):
        parts.append(back_to(*(after(shaped, parts[-1]) if h else shaped), weight_own, h, sent[h]))
    q, p = [v.reshape(4, 2, n // 2, depth) for v in parts]
    gq = swap(pick(q, 1 - zh, 1), "zh")
    gp = send4(lambda k: pick(p, k, 0), "y")
    other_b = swap(after(fb, parts[0]), "c")
    fa, fb = after((fa, fb), parts)
    grad_weight = jnp.zeros(weight.shape, bf16)
    for which, f in ((c, (fa, fb)), (1 - c, (other_a, other_b))):
        grad_weight = lax.dynamic_update_slice_in_dim(
            grad_weight, weight_product(ao, *f), which * half, 1
        )
    sq = pick(q, zh, 1).astype(f32) + gq
    sq16 = sq.astype(bf16)
    sp = total_of(pick(p, y, 0), gp)
    sp, sq16, grad_weight = lax.optimization_barrier((sp, sq16, grad_weight))
    hq = send4(lambda k: pick(sq16, k, 0), "y")
    hp = swap(pick(sp, 1 - zh, 0).astype(bf16), "zh")
    rp = pick(sp, zh, 0) + hp
    rq = total_of(pick(sq, y, 0), hq)
    grad_acts = jnp.concatenate([rq.astype(bf16), rp.astype(bf16)], 0)
    return hidden, grad_acts, grad_weight


def solution(mesh):
    fine = Mesh(mesh.devices.reshape([n for _, n in AXES]), [a for a, _ in AXES])
    row, col = ("y", "zh"), ("zl", "x", "c")
    return jax.shard_map(
        per_device,
        mesh=fine,
        in_specs=(P(row, col), P(col, row), P(col, row)),
        out_specs=(P(col, row), P(row, col), P(col, row)),
        check_vma=False,
    )
```

```python
import math

import jax
import jax.numpy as jnp
from jax import lax
from jax.experimental import pallas as pl
from jax.experimental.layout import Layout, with_layout_constraint
from jax.experimental.pallas import tpu as pltpu
from jax.sharding import Mesh, PartitionSpec as P

scale_c = 0.7978845608028654
cubic_c = 0.044715
f32, bf16 = jnp.float32, jnp.bfloat16

AXES = (("y", 4), ("zh", 2), ("zl", 2), ("x", 4), ("c", 2))
SIZE = dict(AXES)
CHUNKS = (128,)
CUT = 768
VMEM = 12 * 2**20
TILE = 2048
NN, NT, TN = ((1,), (0,)), ((1,), (1,)), ((0,), (0,))
DEPTH_CUT = 384


def gelu_value(v):
    inner = jnp.tanh(scale_c * (v + cubic_c * v * v * v))
    return 0.5 * v * (1.0 + inner)


def gelu_slope(v):
    inner = jnp.tanh(scale_c * (v + cubic_c * v * v * v))
    return 0.5 * (1.0 + inner) + 0.5 * v * (1.0 - inner * inner) * scale_c * (
        1.0 + 3.0 * cubic_c * v * v
    )


def after(value, token):
    return value if token is None else lax.optimization_barrier((value, token))[0]


def shift(value, axis, step):
    n = SIZE[axis]
    return lax.ppermute(value, axis, [(i, (i + step) % n) for i in range(n)])


def pick(value, index, dim):
    return lax.dynamic_index_in_dim(value, index, dim, keepdims=False)


def put(buffer, value, index, dim):
    return lax.dynamic_update_index_in_dim(buffer, value, index, dim)


def send4(block_of, axis, token=None):
    me = lax.axis_index(axis)
    n = SIZE[axis]
    return {s: shift(after(block_of((me + s) % n), token), axis, s) for s in (1, 3, 2)}


def spread4(own, axis, token=None):
    me = lax.axis_index(axis)
    own = after(own, token)
    got = [((me + 4 - s) % 4, shift(own, axis, s)) for s in (1, 3, 2)]
    return [(me, own)] + got


def ring_sum4(block_of, axis):
    me = lax.axis_index(axis)
    far = block_of((me + 2) % 4)
    up, down = shift(far[0], axis, 1), shift(far[1], axis, 3)
    above, below = block_of((me + 1) % 4), block_of((me + 3) % 4)
    above = jnp.stack([(above[0].astype(f32) + up).astype(bf16), above[1]])
    below = jnp.stack([below[0], (below[1].astype(f32) + down).astype(bf16)])
    return block_of(me).astype(f32) + shift(above, axis, 1) + shift(below, axis, 3)


def swap(value, axis, token=None):
    return shift(after(value, token), axis, 1)


def total_of(own, got):
    return own.astype(f32) + got[1] + got[3] + got[2]


def call(kernel, out, ins, flops):
    whole = pl.BlockSpec(memory_space=pltpu.VMEM)
    moved = sum(v.size * v.dtype.itemsize for v in ins)
    return pl.pallas_call(
        kernel,
        out_shape=jax.ShapeDtypeStruct(out, bf16),
        in_specs=[whole] * len(ins),
        out_specs=whole,
        compiler_params=pltpu.CompilerParams(vmem_limit_bytes=VMEM),
        cost_estimate=pl.CostEstimate(flops=flops, bytes_accessed=moved, transcendentals=0),
    )(*ins)


def row_major(value):
    return with_layout_constraint(value, Layout(tuple(range(value.ndim))))


def dot(a, b, dims):
    return lax.dot_general(a, b, (dims, ((), ())), preferred_element_type=f32)


def project(own, sib, weight, weight_sib, low, high):
    rows, depth = own.shape
    m = math.gcd(rows, TILE)

    def kernel(a_ref, b_ref, w_ref, v_ref, o_ref):
        def step(i, carry):
            at = pl.ds(pl.multiple_of(i * m, m), m)
            total = dot(a_ref[at], w_ref[:, low:high], NN) + dot(b_ref[at], v_ref[:, low:high], NN)
            o_ref[at] = total.astype(bf16)
            return carry

        lax.fori_loop(0, rows // m, step, 0)

    flops = 4 * rows * depth * (high - low)
    return call(kernel, (rows, high - low), (own, sib, weight, weight_sib), flops)


def back_to(fa, fb, weight, part, add=None):
    blocks, rows, cut = fa.shape
    depth = weight.shape[0]
    rows = rows // 2
    group = max(1, min(blocks, TILE // rows))

    def kernel(a_ref, b_ref, w_ref, *refs):
        def step(i, carry):
            at = pl.ds(i * group, group)
            here = pl.ds(part * rows, rows)
            a = a_ref[at, here].reshape(group * rows, cut)
            b = b_ref[at, here].reshape(group * rows, fb.shape[2])
            total = dot(a, w_ref[:, :cut], NT) + dot(b, w_ref[:, cut:], NT)
            if add is not None:
                total = total + refs[0][at].reshape(group * rows, depth)
            refs[-1][at] = total.astype(bf16).reshape(group, rows, depth)
            return carry

        lax.fori_loop(0, blocks // group, step, 0)

    ins = (fa, fb, weight) if add is None else (fa, fb, weight, add)
    return call(kernel, (blocks, rows, depth), ins, 2 * blocks * rows * depth * weight.shape[1])


def weight_product(acts, fa, fb):
    depth, cut = acts.shape[1], fa.shape[1]

    def kernel(t_ref, a_ref, b_ref, o_ref):
        o_ref[:, :cut] = dot(t_ref[...], a_ref[...], TN).astype(bf16)
        o_ref[:, cut:] = dot(t_ref[...], b_ref[...], TN).astype(bf16)

    width = cut + fb.shape[1]
    return call(kernel, (depth, width), (acts, fa, fb), 2 * acts.size * width)


def per_device(acts, weight, cotangent):
    rows, depth = acts.shape
    half = weight.shape[1] // 2
    cut, dcut = CUT, DEPTH_CUT
    zl, x, zh, y, c = (lax.axis_index(a) for a in ("zl", "x", "zh", "y", "c"))

    def unit_half(value, which):
        return lax.dynamic_slice_in_dim(value, which * half, half, 1)

    acts_two = acts.reshape(2, rows // 2, depth)
    starts = [sum(CHUNKS[:j]) for j in range(len(CHUNKS))]

    def gather_acts(j):
        size = CHUNKS[j]
        n = 2 * size
        own = acts_two[:, starts[j] : starts[j] + size].reshape(n, depth)
        mine = jnp.zeros((4, 2, n, depth), bf16)
        pa, pb = own[:, :dcut], own[:, dcut:]
        other = swap(pb, "zh")
        weight_own = unit_half(after(weight, other), c)
        four = jnp.zeros((4, n, dcut), bf16)
        blocks = spread4(pa, "y")
        for place, block in blocks:
            four = put(four, block, place, 0)
        weight_sib = swap(unit_half(after(weight, [v for _, v in blocks]), 1 - c), "c")
        pair = put(put(jnp.zeros((2, n, depth - dcut), bf16), pb, zh, 0), other, 1 - zh, 0)
        four_other = after(swap(four, "zh"), weight_sib)
        for place, block in spread4(pair, "y"):
            mine = lax.dynamic_update_slice(mine, block[None], (place, 0, 0, dcut))
        mine = lax.dynamic_update_slice(mine, four[:, None], (0, zh, 0, 0))
        mine = lax.dynamic_update_slice(mine, four_other[:, None], (0, 1 - zh, 0, 0))
        mine = row_major(mine.reshape(8 * n, depth))
        return mine, row_major(swap(mine, "c")), weight_own, weight_sib

    cot_two = jnp.zeros((2, rows // 2, half), bf16)
    cot_two = put(cot_two, unit_half(cotangent, c), c, 0)
    cot_two = put(cot_two, swap(unit_half(cotangent, 1 - c), "c"), 1 - c, 0)

    ao, ab, weight_own, weight_sib = gather_acts(0)
    hidden_own, hidden_sib, full = [], [], []
    xt = zt = None
    for j, size in enumerate(CHUNKS):
        n = 2 * size

        pb = project(ao, ab, weight_own, weight_sib, cut, half).reshape(2, 4, n, half - cut)
        gb = swap(pick(pb, 1 - zl, 0), "zl", zt)
        pa = project(ao, ab, weight_own, weight_sib, 0, cut).reshape(2, 4, n, cut)
        sb = pick(pb, zl, 0).astype(f32) + gb
        sb16 = sb.astype(bf16)
        sa = ring_sum4(lambda k: pick(pa, k, 1), "x")
        qb = send4(lambda k: pick(sb16, k, 0), "x")
        qa = swap(pick(sa, 1 - zl, 0).astype(bf16), "zl")
        pre_a = pick(sa, zl, 0) + qa
        pre_b = total_of(pick(sb, x, 0), qb)

        cot = cot_two[:, starts[j] : starts[j] + size].reshape(n, half)
        ba = (cot[:, :cut].astype(f32) * gelu_slope(pre_a)).astype(bf16)
        bb = (cot[:, cut:].astype(f32) * gelu_slope(pre_b)).astype(bf16)
        hid = jnp.concatenate([gelu_value(pre_a), gelu_value(pre_b)], 1).astype(bf16)
        hid = hid.reshape(2, size, half)
        hidden_own.append(pick(hid, c, 0))
        hidden_sib.append(pick(hid, 1 - c, 0))

        ra = swap(ba, "zl")
        pieces = spread4(bb, "x")
        first = swap(bb, "zl")
        rest = swap(jnp.stack([v for _, v in pieces[1:]]), "zl")
        fb = jnp.zeros((2, 4, n, half - cut), bf16)
        for k, (place, block) in enumerate(pieces):
            fb = lax.dynamic_update_slice(fb, block[None, None], (zl, place, 0, 0))
            got = first if k == 0 else rest[k - 1]
            fb = lax.dynamic_update_slice(fb, got[None, None], (1 - zl, place, 0, 0))
        pair = put(put(jnp.zeros((2, n, cut), bf16), ba, zl, 0), ra, 1 - zl, 0)
        fa = jnp.zeros((2, 4, n, cut), bf16)
        low, high = shift(pair, "x", 1), shift(pair, "x", 3)
        far0, far1 = shift(low[0], "x", 1), shift(high[1], "x", 3)
        for place, block in ((x, pair), ((x + 3) % 4, low), ((x + 1) % 4, high)):
            fa = put(fa, block, place, 1)
        for k, block in enumerate((far0, far1)):
            fa = lax.dynamic_update_slice(fa, block[None, None], (k, (x + 2) % 4, 0, 0))
        full.append((fa.reshape(8 * n, cut), fb.reshape(8 * n, half - cut)))

    hid_other = swap(jnp.concatenate(hidden_sib, 0), "c")
    hidden = jnp.zeros(cotangent.shape, bf16)
    hidden = lax.dynamic_update_slice_in_dim(hidden, jnp.concatenate(hidden_own, 0), c * half, 1)
    hidden = lax.dynamic_update_slice_in_dim(hidden, hid_other, (1 - c) * half, 1)

    fa, fb = after(full[0], hid_other)
    n = 2 * CHUNKS[0]
    shaped = [v.reshape(8, n, -1) for v in (fa, fb)]
    other_a = swap(fa, "c")
    sent = [swap(back_to(*shaped, weight_sib, h), "c") for h in range(2)]
    parts = []
    for h in range(2):
        parts.append(back_to(*(after(shaped, parts[-1]) if h else shaped), weight_own, h, sent[h]))
    q, p = [v.reshape(4, 2, n // 2, depth) for v in parts]
    gq = swap(pick(q, 1 - zh, 1), "zh")
    gp = send4(lambda k: pick(p, k, 0), "y")
    other_b = swap(after(fb, parts[0]), "c")
    fa, fb = after((fa, fb), parts)
    grad_weight = jnp.zeros(weight.shape, bf16)
    for which, f in ((c, (fa, fb)), (1 - c, (other_a, other_b))):
        grad_weight = lax.dynamic_update_slice_in_dim(
            grad_weight, weight_product(ao, *f), which * half, 1
        )
    sq = pick(q, zh, 1).astype(f32) + gq
    sq16 = sq.astype(bf16)
    sp = total_of(pick(p, y, 0), gp)
    sp, sq16, grad_weight = lax.optimization_barrier((sp, sq16, grad_weight))
    hq = send4(lambda k: pick(sq16, k, 0), "y")
    hp = swap(pick(sp, 1 - zh, 0).astype(bf16), "zh")
    rp = pick(sp, zh, 0) + hp
    rq = total_of(pick(sq, y, 0), hq)
    grad_acts = jnp.concatenate([rq.astype(bf16), rp.astype(bf16)], 0)
    return hidden, grad_acts, grad_weight


def solution(mesh):
    fine = Mesh(mesh.devices.reshape([n for _, n in AXES]), [a for a, _ in AXES])
    row, col = ("y", "zh"), ("zl", "x", "c")
    return jax.shard_map(
        per_device,
        mesh=fine,
        in_specs=(P(row, col), P(col, row), P(col, row)),
        out_specs=(P(col, row), P(row, col), P(col, row)),
        check_vma=False,
    )
```
